32 devices in a mesh: sx: 8 (over y, x, core), sy: 4 (over z).
Axes of the slice: x: 2, y: 2, z: 4, core: 2. Of those that a mesh axis runs over, the one named last changes fastest.
Arguments:
- volume: bfloat16 [32, 128, 1024], P(None, 'sx', 'sy'), may hold values from -6 to 6
- w_first: bfloat16 [27, 32, 32], replicated, may hold values from -0.21875 to 0.21875
- down_weight: bfloat16 [2048, 128], replicated, may hold values from -0.125 to 0.125
- w_coarse: bfloat16 [4, 27, 128, 128], replicated, may hold values from -0.15625 to 0.15625
- w_up: bfloat16 [128, 2048], replicated, may hold values from -0.5 to 0.5
- closing_weight: bfloat16 [27, 32, 64], replicated, may hold values from -0.21875 to 0.21875
Outputs:
- result: bfloat16 [32, 128, 1024], P(None, 'sx', 'sy')
The draws below stay inside these ranges and needn't reach their ends.
All inputs are finite; a program needn't handle non-finite values.
Results may differ from the reference program's by a relative error of at most 0.0095.
Values may be sent and summed in bfloat16 or wider, within the bound.
A program may use at most 64 MiB of HBM per device.

```python
import jax
import jax.numpy as jnp
from jax import lax

C = 32
CC = 128
LAYERS = 4
NZ = 16
NX = 128
NY = 64


def level_of(rng, dims, cuts, least, high):
    factor_of = 1.0
    for position, shards_of in cuts:
        heights = jax.random.uniform(jax.random.fold_in(jax.random.fold_in(rng, 6), position), (shards_of,), jnp.float32, least / len(cuts), high / len(cuts))
        factor_of = factor_of * jnp.repeat(jnp.exp(heights), dims[position] // shards_of).reshape((-1,) + (1,) * (len(dims) - 1 - position))
    return factor_of


def normal_values(key, extent, spread, limit, split=(), kind=jnp.bfloat16):
    values = spread * jax.random.normal(key, extent, jnp.float32)
    if split:
        values = values * level_of(key, extent, split, -0.22, 0.18)
    return jnp.clip(values, -limit, limit).astype(kind)


def setup_inputs(seed: int = 0) -> dict:
    keys = jax.random.split(jax.random.key(seed), 7)
    volume = normal_values(keys[0], (C, NX, NY * NZ), 1.0, 6.0, ((1, 8), (2, 4)))
    w_first = normal_values(keys[1], (27, C, C), (27 * C) ** -0.5, 0.21875)
    down_weight = normal_values(keys[2], (64 * C, CC), (64 * C) ** -0.5, 0.125)
    w_coarse = normal_values(keys[3], (LAYERS, 27, CC, CC), (27 * CC // 2) ** -0.5, 0.15625)
    w_up = normal_values(keys[4], (CC, 64 * C), CC ** -0.5, 0.5)
    closing_weight = normal_values(keys[5], (27, C, 2 * C), (27 * C) ** -0.5, 0.21875)
    return {"volume": volume, "w_first": w_first, "down_weight": down_weight, "w_coarse": w_coarse, "w_up": w_up, "closing_weight": closing_weight}


def conv_same(grid_field, weight):
    out_width = weight.shape[1]
    in_width = weight.shape[2]
    kernel = weight.astype(jnp.float32).reshape(3, 3, 3, out_width, in_width).transpose(3, 4, 0, 1, 2)
    summed = lax.conv_general_dilated(grid_field.astype(jnp.float32)[None], kernel, (1, 1, 1), ((1, 1), (1, 1), (1, 1)), dimension_numbers=("NCDHW", "OIDHW", "NCDHW"), precision=lax.Precision.HIGHEST)
    return summed[0]


def reference(volume, w_first, down_weight, w_coarse, w_up, closing_weight):
    grid_field = volume.reshape(C, NX, NY, NZ)
    skip_features = jax.nn.relu(conv_same(grid_field, w_first)).astype(jnp.bfloat16)
    blocks = skip_features.reshape(C, NX // 4, 4, NY // 4, 4, NZ // 4, 4).transpose(1, 3, 5, 0, 2, 4, 6).reshape(-1, C * 64)
    coarse_features = jnp.dot(blocks, down_weight, preferred_element_type=jnp.float32).astype(jnp.bfloat16)
    coarse_features = coarse_features.reshape(NX // 4, NY // 4, NZ // 4, CC).transpose(3, 0, 1, 2)
    for layer_index in range(LAYERS):
        coarse_features = jax.nn.relu(conv_same(coarse_features, w_coarse[layer_index])).astype(jnp.bfloat16)
    coarse_cells = coarse_features.transpose(1, 2, 3, 0).reshape(-1, CC)
    upsampled = jnp.dot(coarse_cells, w_up, preferred_element_type=jnp.float32).astype(jnp.bfloat16)
    upsampled = upsampled.reshape(NX // 4, NY // 4, NZ // 4, C, 4, 4, 4).transpose(3, 0, 4, 1, 5, 2, 6).reshape(C, NX, NY, NZ)
    joined = jnp.concatenate([skip_features, upsampled], axis=0)
    final = conv_same(joined, closing_weight).astype(jnp.bfloat16)
    return final.reshape(C, NX, NY * NZ)
```

```python
import functools

import jax
import jax.numpy as jnp
from jax import lax
from jax.experimental import pallas as pl
from jax.experimental.pallas import tpu as pltpu
from jax.sharding import PartitionSpec as P

NZ = 16
S = 4
F32 = jnp.float32
BF = jnp.bfloat16
DIRS = [(dx, dy) for dx in (-1, 0, 1) for dy in (-1, 0, 1) if (dx, dy) != (0, 0)]
OPP = [DIRS.index((-dx, -dy)) for dx, dy in DIRS]
NT = (((1,), (1,)), ((), ()))
TN = (((0,), (0,)), ((), ()))


def dot(a, b, dims=(((1,), (0,)), ((), ()))):
    return lax.dot_general(a, b, dims, preferred_element_type=F32)


def banded(w, part, width):
    taps, out, inner = w.shape
    lanes = 2 * S * width
    shape = (inner, S * lanes)
    channel = lax.broadcasted_iota(jnp.int32, shape, 0)
    column = lax.broadcasted_iota(jnp.int32, shape, 1)
    zo = column // lanes
    lane = column % lanes
    quarter = lane // width
    zi = jnp.where(quarter < S, quarter, jnp.where(quarter == S, S, jnp.where(quarter == 2 * S - 1, -1, 99)))
    same = channel == lane % width + part * width
    w4 = w.reshape(taps // 3, 3, out, inner)
    total = None
    for tz in range(3):
        pick = jnp.where(same & (zi - zo + 1 == tz), 1.0, 0.0).astype(BF)
        term = dot(w4[:, tz].reshape(-1, inner), pick)
        total = term if total is None else total + term
    total = total.astype(BF).reshape(taps // 3, out, S * lanes)
    rows = [total[:, :, z * lanes : (z + 1) * lanes] for z in range(S)]
    return jnp.concatenate(rows, axis=1)


def spread(f_ref, a_ref, bx, rows, width, lo=0, hi=None):
    lanes = S * width
    hi = bx + 2 if hi is None else hi

    def step(x, carry):
        zb = lax.broadcasted_iota(jnp.int32, (rows, lanes), 0) % S
        lane = lax.broadcasted_iota(jnp.int32, (rows, lanes), 1)
        from_prev = (lane >= lanes - width) & (zb != 0)
        from_next = (lane < width) & (zb != S - 1)
        for dy in range(3):
            start = 4 + S * dy
            own = f_ref[x, start : start + rows, :]
            prev = f_ref[x, start - 1 : start - 1 + rows, :]
            after = f_ref[x, start + 1 : start + 1 + rows, :]
            edge = jnp.where(from_prev, prev, jnp.where(from_next, after, 0.0))
            a_ref[x, :, 2 * dy * lanes : (2 * dy + 1) * lanes] = own.astype(BF)
            a_ref[x, :, (2 * dy + 1) * lanes : (2 * dy + 2) * lanes] = edge.astype(BF)
        return carry

    lax.fori_loop(lo, hi, step, 0)


def fine(a_ref, b_ref, bx, rows):
    total = None
    for dx in range(3):
        a = a_ref[dx : dx + bx].reshape(bx * rows, a_ref.shape[2])
        term = dot(a, b_ref[dx], NT)
        total = term if total is None else total + term
    return total


def kernel(
    axes, x_ref, wf_ref, dw_ref, wc_hbm, up_ref, cw_ref, out_ref,
    f_ref, s_ref, a_ref, b1_ref, b2_ref, b3_ref, acc_ref, t_ref, c_ref, d_ref, wc_ref,
    send_f, recv_f, send_c, recv_c, wsem, ssem_f, rsem_f, ssem_c, rsem_c,
):
    ax, ay = axes
    nx, ny = lax.axis_size(ax), lax.axis_size(ay)
    ix, iy = lax.axis_index(ax), lax.axis_index(ay)
    bx, width, flat = x_ref.shape
    by = flat // NZ
    lanes = S * width
    rows = by * (NZ // S)
    ca, cb = bx // S, by // S
    cc = wc_ref.shape[2]
    layers = wc_ref.shape[0]
    crow = cb * S
    edge = bx * S

    weights = pltpu.make_async_copy(wc_hbm, wc_ref, wsem)
    weights.start()

    def exists(d):
        dx, dy = DIRS[d]
        ok = ix >= 0
        if dx:
            ok = ok & (ix + dx >= 0) & (ix + dx < nx)
        if dy:
            ok = ok & (iy + dy >= 0) & (iy + dy < ny)
        return ok

    def target(d):
        dx, dy = DIRS[d]
        return (ix + dx, iy + dy)

    barrier = pltpu.get_barrier_semaphore()
    for d in range(8):
        @pl.when(exists(d))
        def _(d=d):
            pl.semaphore_signal(barrier, inc=1, device_id=target(d), device_id_type=pl.DeviceIdType.MESH)

    def fine_copy(phase, d):
        count = 16 if DIRS[d][0] and DIRS[d][1] else (rows if DIRS[d][0] else edge)
        return pltpu.make_async_remote_copy(
            src_ref=send_f.at[phase, d, pl.ds(0, count)],
            dst_ref=recv_f.at[phase, OPP[d], pl.ds(0, count)],
            send_sem=ssem_f.at[phase, d],
            recv_sem=rsem_f.at[phase, OPP[d]],
            device_id=target(d),
            device_id_type=pl.DeviceIdType.MESH,
        )

    def coarse_copy(phase, d):
        return pltpu.make_async_remote_copy(
            src_ref=send_c.at[phase],
            dst_ref=recv_c.at[phase, OPP[d]],
            send_sem=ssem_c.at[phase, d],
            recv_sem=rsem_c.at[phase, OPP[d]],
            device_id=target(d),
            device_id_type=pl.DeviceIdType.MESH,
        )

    def each(make, act):
        for d in range(8):
            @pl.when(exists(d))
            def _(d=d):
                act(make(d), d)

    def start_all(make):
        each(make, lambda c, d: c.start())

    def sent_all(make):
        each(make, lambda c, d: c.wait_send())

    def recv_wait(copy_of):
        for d in range(8):
            @pl.when(exists(d))
            def _(d=d):
                copy_of(d).wait_recv()

    def fine_arrival(phase):
        def make(d):
            count = 16 if DIRS[d][0] and DIRS[d][1] else (rows if DIRS[d][0] else edge)
            return pltpu.make_async_remote_copy(
                src_ref=send_f.at[phase, d, pl.ds(0, count)],
                dst_ref=recv_f.at[phase, d, pl.ds(0, count)],
                send_sem=ssem_f.at[phase, d],
                recv_sem=rsem_f.at[phase, d],
                device_id=target(d),
                device_id_type=pl.DeviceIdType.MESH,
            )
        return make

    def coarse_arrival(phase):
        def make(d):
            return pltpu.make_async_remote_copy(
                src_ref=send_c.at[phase],
                dst_ref=recv_c.at[phase, d],
                send_sem=ssem_c.at[phase, d],
                recv_sem=rsem_c.at[phase, d],
                device_id=target(d),
                device_id_type=pl.DeviceIdType.MESH,
            )
        return make

    for d in range(8):
        @pl.when(jnp.logical_not(exists(d)))
        def _(d=d):
            recv_f[:, d] = jnp.zeros(recv_f.shape[:1] + recv_f.shape[2:], BF)
            recv_c[:, d] = jnp.zeros(recv_c.shape[:1] + recv_c.shape[2:], BF)

    def pack(ref, phase):
        t_ref[...] = jnp.zeros_like(t_ref)
        for d, (dx, dy) in enumerate(DIRS):
            x = 1 if dx < 0 else bx
            r = 8 if dy < 0 else 8 + rows - S
            if dx and dy:
                t_ref[d, 0:S] = ref[x, r : r + S]
            elif dy:
                for i in range(bx):
                    t_ref[d, S * i : S * (i + 1)] = ref[i + 1, r : r + S]
            if dx and not dy:
                send_f[phase, d, 0:rows] = ref[x, 8 : 8 + rows].astype(BF)
            else:
                send_f[phase, d] = t_ref[d].astype(BF)

    def unpack(ref, phase):
        for d, (dx, dy) in enumerate(DIRS):
            x = 0 if dx < 0 else bx + 1
            r = 4 if dy < 0 else 8 + rows
            if dx and not dy:
                ref[x, 8 : 8 + rows] = recv_f[phase, d, 0:rows].astype(F32)
            elif dx:
                ref[x, r : r + S] = recv_f[phase, d, 0:16].astype(F32)[0:S]
            else:
                t_ref[d, 0:edge] = recv_f[phase, d, 0:edge].astype(F32)
                for i in range(bx):
                    ref[i + 1, r : r + S] = t_ref[d, S * i : S * (i + 1)]

    group_r = lax.broadcasted_iota(jnp.int32, (rows, flat), 0)
    group_c = lax.broadcasted_iota(jnp.int32, (rows, flat), 1)
    select = jnp.where(group_c // S == group_r, 1.0, 0.0).astype(BF)
    quarter = lax.broadcasted_iota(jnp.int32, (lanes, flat), 0) // width
    in_quarter = (lax.broadcasted_iota(jnp.int32, (lanes, flat), 1) % S == quarter).astype(F32).astype(BF)
    for x in range(bx):
        one = x_ref[x]
        four = jnp.concatenate([one] * S, axis=0) * in_quarter
        f_ref[x + 1, 8 : 8 + rows] = dot(select, four, NT)

    pack(f_ref, 0)
    neighbours = sum(jnp.where(exists(d), 1, 0) for d in range(8))
    pl.semaphore_wait(barrier, neighbours)
    start_all(functools.partial(fine_copy, 0))

    def store_banded(ref, value):
        for k in range(9):
            ref[k // 3, :, (k % 3) * 2 * lanes : (k % 3 + 1) * 2 * lanes] = value[k]

    store_banded(b1_ref, banded(wf_ref[...], 0, width))
    store_banded(b2_ref, banded(cw_ref[...], 0, width))
    store_banded(b3_ref, banded(cw_ref[...], 1, width))

    recv_wait(fine_arrival(0))
    unpack(f_ref, 0)
    spread(f_ref, a_ref, bx, rows, width)
    skip = jnp.maximum(fine(a_ref, b1_ref, bx, rows), 0.0).astype(BF).astype(F32)
    s_ref[1 : bx + 1, 8 : 8 + rows] = skip.reshape(bx, rows, lanes)
    pack(s_ref, 1)
    start_all(functools.partial(fine_copy, 1))

    pieces = []
    for ox in range(S):
        for half in range(2):
            group = []
            for a in range(ca):
                for b in range(cb):
                    r = 8 + b * S * S + half * 2 * S
                    group.append(s_ref[1 + S * a + ox, r : r + 2 * S])
            pieces.append(jnp.concatenate(group, axis=0).astype(BF))
    lhs = jnp.concatenate(pieces, axis=1)
    down = []
    for parity in range(2):
        down.append(
            jnp.concatenate([dw_ref[S * ox + 2 * half + parity] for ox in range(S) for half in range(2)], axis=0)
        )
    both = [dot(lhs, w).reshape(ca * cb, 2 * S, cc) for w in down]
    t_down = both[0][:, 0:S] + both[1][:, S : 2 * S]
    for a in range(ca):
        for b in range(cb):
            d_ref[a, S * b : S * (b + 1)] = t_down[a * cb + b]
    send_c[0] = d_ref[...].reshape(ca * crow, cc).astype(BF)
    start_all(functools.partial(coarse_copy, 0))

    recv_wait(fine_arrival(1))
    unpack(s_ref, 1)
    spread(s_ref, a_ref, bx, rows, width)
    acc_ref[...] = fine(a_ref, b2_ref, bx, rows)

    weights.wait()
    recv_wait(coarse_arrival(0))

    def place(phase):
        for d, (dx, dy) in enumerate(DIRS):
            c_ref[ca * (dx + 1) : ca * (dx + 2), 8 + crow * (dy + 1) : 8 + crow * (dy + 2)] = (
                recv_c[phase, d].astype(F32).reshape(ca, crow, cc)
            )
        c_ref[ca : 2 * ca, 8 + crow : 8 + 2 * crow] = send_c[phase].astype(F32).reshape(ca, crow, cc)

    place(0)
    for layer in range(layers):
        margin = layers - 1 - layer
        na, nb = ca + 2 * margin, cb + 2 * margin
        n = nb * S
        off = layer
        zb = lax.broadcasted_iota(jnp.int32, (na, n, cc), 1) % S
        taps = []
        for da in range(3):
            for db in range(3):
                for dz in range(3):
                    r = 8 + S * (off + db) + dz - 1
                    v = c_ref[off + da : off + da + na, r : r + n]
                    if dz == 0:
                        v = jnp.where(zb != 0, v, 0.0)
                    if dz == 2:
                        v = jnp.where(zb != S - 1, v, 0.0)
                    taps.append(v.astype(BF).reshape(na * n, cc))
        lhs = jnp.concatenate(taps, axis=1)
        rhs = jnp.concatenate([wc_ref[layer, t] for t in range(27)], axis=1)
        summed = jnp.maximum(dot(lhs, rhs, NT), 0.0).reshape(na, n, cc)
        ga = lax.broadcasted_iota(jnp.int32, (na, n, cc), 0) + ix * ca - margin
        gb = lax.broadcasted_iota(jnp.int32, (na, n, cc), 1) // S + iy * cb - margin
        keep = (ga >= 0) & (ga < nx * ca) & (gb >= 0) & (gb < ny * cb)
        summed = jnp.where(keep, summed, 0.0).astype(BF).astype(F32)
        c_ref[off + 1 : off + 1 + na, 8 + S * (off + 1) : 8 + S * (off + 1) + n] = summed
    send_c[1] = c_ref[ca : 2 * ca, 8 + crow : 8 + 2 * crow].reshape(ca * crow, cc).astype(BF)
    start_all(functools.partial(coarse_copy, 1))
    recv_wait(coarse_arrival(1))
    place(1)

    cells = c_ref[ca - 1 : 2 * ca + 1, 8 + crow - S : 8 + 2 * crow + S]
    cells = cells.reshape((ca + 2) * (crow + 2 * S), cc).astype(BF)
    for ox in range(S):
        for oy in range(S):
            up = dot(cells, up_ref[S * ox + oy], NT).astype(BF).astype(F32)
            up = up.reshape(ca + 2, crow + 2 * S, lanes)
            for a in range(ca + 2):
                x = S * (a - 1) + ox + 1
                if x < 0 or x > bx + 1:
                    continue
                for b in range(cb + 2):
                    y = S * (b - 1) + oy
                    if y < -1 or y > by:
                        continue
                    f_ref[x, 8 + S * y : 8 + S * (y + 1)] = up[a, S * b : S * (b + 1)]

    spread(f_ref, a_ref, bx, rows, width)
    total = (acc_ref[...] + fine(a_ref, b3_ref, bx, rows)).astype(BF)
    for x in range(bx):
        one = dot(total[x * rows : (x + 1) * rows], select, TN)
        picked = jnp.where(in_quarter > 0, one, 0.0)
        res = picked[0:width]
        for z in range(1, S):
            res = res + picked[z * width : (z + 1) * width]
        out_ref[x] = res.astype(BF)

    for phase in range(2):
        sent_all(functools.partial(fine_copy, phase))
        sent_all(functools.partial(coarse_copy, phase))


def local(volume, w_first, down_weight, w_coarse, w_up, closing_weight):
    width, bx, flat = volume.shape
    by = flat // NZ
    lanes = S * width
    rows = by * (NZ // S)
    ca, crow = bx // S, by // S * S
    layers, _, cc, _ = w_coarse.shape
    cube = S * S * S
    down = down_weight.reshape(width, cube, cc).transpose(1, 0, 2).reshape(S * S, lanes, cc)
    up = w_up.T.reshape(width, cube, cc).transpose(1, 0, 2).reshape(S * S, lanes, cc)
    slot = max(rows, S * bx)
    vmem = pl.BlockSpec(memory_space=pltpu.VMEM)
    out = pl.pallas_call(
        functools.partial(kernel, ("sx", "sy")),
        out_shape=jax.ShapeDtypeStruct((bx, width, flat), BF),
        in_specs=[vmem, vmem, vmem, pl.BlockSpec(memory_space=pl.ANY), vmem, vmem],
        out_specs=vmem,
        scratch_shapes=[
            pltpu.VMEM((bx + 2, rows + 16, lanes), F32),
            pltpu.VMEM((bx + 2, rows + 16, lanes), F32),
            pltpu.VMEM((bx + 2, rows, 6 * lanes), BF),
            pltpu.VMEM((3, lanes, 6 * lanes), BF),
            pltpu.VMEM((3, lanes, 6 * lanes), BF),
            pltpu.VMEM((3, lanes, 6 * lanes), BF),
            pltpu.VMEM((bx * rows, lanes), F32),
            pltpu.VMEM((8, slot, lanes), F32),
            pltpu.VMEM((3 * ca, 3 * crow + 16, cc), F32),
            pltpu.VMEM((ca, crow, cc), F32),
            pltpu.VMEM(w_coarse.shape, BF),
            pltpu.VMEM((2, 8, slot, lanes), BF),
            pltpu.VMEM((2, 8, slot, lanes), BF),
            pltpu.VMEM((2, ca * crow, cc), BF),
            pltpu.VMEM((2, 8, ca * crow, cc), BF),
            pltpu.SemaphoreType.DMA,
            pltpu.SemaphoreType.DMA((2, 8)),
            pltpu.SemaphoreType.DMA((2, 8)),
            pltpu.SemaphoreType.DMA((2, 8)),
            pltpu.SemaphoreType.DMA((2, 8)),
        ],
        compiler_params=pltpu.CompilerParams(
            collective_id=0, has_side_effects=True, vmem_limit_bytes=48 * 1024 * 1024
        ),
    )(volume.transpose(1, 0, 2), w_first, down, w_coarse, up, closing_weight)
    return out.transpose(1, 0, 2)


def solution(mesh):
    return jax.shard_map(
        local,
        mesh=mesh,
        in_specs=(P(None, "sx", "sy"), P(), P(), P(), P(), P()),
        out_specs=P(None, "sx", "sy"),
        check_vma=False,
    )
```

```python
import functools

import jax
import jax.numpy as jnp
from jax import lax
from jax.experimental import pallas as pl
from jax.experimental.pallas import tpu as pltpu
from jax.sharding import PartitionSpec as P

NZ = 16
S = 4
F32 = jnp.float32
BF = jnp.bfloat16
DIRS = [(dx, dy) for dx in (-1, 0, 1) for dy in (-1, 0, 1) if (dx, dy) != (0, 0)]
OPP = [DIRS.index((-dx, -dy)) for dx, dy in DIRS]
NT = (((1,), (1,)), ((), ()))
TN = (((0,), (0,)), ((), ()))


def dot(a, b, dims=(((1,), (0,)), ((), ()))):
    return lax.dot_general(a, b, dims, preferred_element_type=F32)


def banded(w, part, width):
    taps, out, inner = w.shape
    lanes = S * width
    shape = (inner, 2 * S * lanes)
    channel = lax.broadcasted_iota(jnp.int32, shape, 0)
    column = lax.broadcasted_iota(jnp.int32, shape, 1)
    block = column // lanes
    zi = column % lanes // width
    zo = jnp.where(block < S, block, jnp.where(block == S, S, jnp.where(block == 2 * S - 1, -1, 99)))
    same = channel == column % width + part * width
    w4 = w.reshape(taps // 3, 3, out, inner)
    total = None
    for tz in range(3):
        pick = jnp.where(same & (zi - zo + 1 == tz), 1.0, 0.0).astype(BF)
        term = dot(w4[:, tz].reshape(-1, inner), pick)
        total = term if total is None else total + term
    total = total.astype(BF).reshape(taps // 3, out, 2 * S * lanes)
    rows = [total[:, :, z * lanes : (z + 1) * lanes] for z in range(2 * S)]
    return jnp.concatenate(rows, axis=1)


def windows(v_ref, rows, *lead):
    return [v_ref[(*lead, slice(4 + S * k, 4 + S * k + rows))].astype(BF) for k in range(3)]


def spread(f_ref, a_ref, rows, lanes, lo, hi):
    def step(x, carry):
        for k, v in enumerate(windows(f_ref, rows, x)):
            a_ref[x, :, k * lanes : (k + 1) * lanes] = v
        return carry

    lax.fori_loop(lo, hi, step, 0)


def fine(a_ref, b_ref, bx, rows):
    a = jnp.concatenate([a_ref[k : k + bx].reshape(bx * rows, a_ref.shape[2]) for k in range(3)], axis=1)
    b = jnp.concatenate([b_ref[k] for k in range(3)], axis=1)
    return dot(a, b, NT)


def joined_z(total, lanes, width):
    n = total.shape[0]
    own, other = total[:, :lanes], total[:, lanes:]
    zb = lax.broadcasted_iota(jnp.int32, (n, lanes), 0) % S
    lane = lax.broadcasted_iota(jnp.int32, (n, lanes), 1)
    down = pltpu.roll(other, 1, 0)
    up = pltpu.roll(other, n - 1, 0)
    first = (lane < width) & (zb != 0)
    last = (lane >= lanes - width) & (zb != S - 1)
    return own + jnp.where(first, down, jnp.where(last, up, 0.0))


def kernel(
    axes, x_hbm, wf_hbm, dw_hbm, wc_hbm, up_hbm, cw_hbm, out_ref,
    x_ref, wf_ref, dwo_ref, wc_ref, upo_ref, cw_ref,
    v_ref, perm_ref, dw_ref, up_ref, f_ref, s_ref, a_ref, b1_ref, b2_ref, b3_ref, acc_ref, t_ref, h_ref,
    c_ref, d_ref, o_ref, send_f, recv_f, send_c, recv_c, wsem, ssem_f, rsem_f, ssem_c, rsem_c,
):
    ax, ay = axes
    nx, ny = lax.axis_size(ax), lax.axis_size(ay)
    ix, iy = lax.axis_index(ax), lax.axis_index(ay)
    width, bx, flat = x_ref.shape
    by = flat // NZ
    lanes = S * width
    rows = by * (NZ // S)
    ca, cb = bx // S, by // S
    cc = wc_ref.shape[2]
    layers = wc_ref.shape[0]
    crow = cb * S
    edge = bx * S

    pairs = [(x_hbm, x_ref), (wf_hbm, wf_ref), (cw_hbm, cw_ref), (dw_hbm, dwo_ref), (up_hbm, upo_ref), (wc_hbm, wc_ref)]
    loads = [pltpu.make_async_copy(src, dst, wsem.at[k]) for k, (src, dst) in enumerate(pairs)]
    for load in loads:
        load.start()

    def exists(d):
        dx, dy = DIRS[d]
        ok = ix >= 0
        if dx:
            ok = ok & (ix + dx >= 0) & (ix + dx < nx)
        if dy:
            ok = ok & (iy + dy >= 0) & (iy + dy < ny)
        return ok

    def target(d):
        dx, dy = DIRS[d]
        return (ix + dx, iy + dy)

    barrier = pltpu.get_barrier_semaphore()
    for d in range(8):
        @pl.when(exists(d))
        def _(d=d):
            pl.semaphore_signal(barrier, inc=1, device_id=target(d), device_id_type=pl.DeviceIdType.MESH)

    def fine_copy(phase, d):
        count = 16 if DIRS[d][0] and DIRS[d][1] else (rows if DIRS[d][0] else edge)
        return pltpu.make_async_remote_copy(
            src_ref=send_f.at[phase, d, pl.ds(0, count)],
            dst_ref=recv_f.at[phase, OPP[d], pl.ds(0, count)],
            send_sem=ssem_f.at[phase, d],
            recv_sem=rsem_f.at[phase, OPP[d]],
            device_id=target(d),
            device_id_type=pl.DeviceIdType.MESH,
        )

    def coarse_copy(phase, d):
        return pltpu.make_async_remote_copy(
            src_ref=send_c.at[phase],
            dst_ref=recv_c.at[phase, OPP[d]],
            send_sem=ssem_c.at[phase, d],
            recv_sem=rsem_c.at[phase, OPP[d]],
            device_id=target(d),
            device_id_type=pl.DeviceIdType.MESH,
        )

    def each(make, act):
        for d in range(8):
            @pl.when(exists(d))
            def _(d=d):
                act(make(d), d)

    def start_all(make):
        each(make, lambda c, d: c.start())

    def sent_all(make):
        each(make, lambda c, d: c.wait_send())

    def recv_wait(copy_of):
        for d in range(8):
            @pl.when(exists(d))
            def _(d=d):
                copy_of(d).wait_recv()

    def fine_arrival(phase):
        def make(d):
            count = 16 if DIRS[d][0] and DIRS[d][1] else (rows if DIRS[d][0] else edge)
            return pltpu.make_async_remote_copy(
                src_ref=send_f.at[phase, d, pl.ds(0, count)],
                dst_ref=recv_f.at[phase, d, pl.ds(0, count)],
                send_sem=ssem_f.at[phase, d],
                recv_sem=rsem_f.at[phase, d],
                device_id=target(d),
                device_id_type=pl.DeviceIdType.MESH,
            )
        return make

    def coarse_arrival(phase):
        def make(d):
            return pltpu.make_async_remote_copy(
                src_ref=send_c.at[phase],
                dst_ref=recv_c.at[phase, d],
                send_sem=ssem_c.at[phase, d],
                recv_sem=rsem_c.at[phase, d],
                device_id=target(d),
                device_id_type=pl.DeviceIdType.MESH,
            )
        return make

    for d in range(8):
        @pl.when(jnp.logical_not(exists(d)))
        def _(d=d):
            recv_f[:, d] = jnp.zeros(recv_f.shape[:1] + recv_f.shape[2:], BF)
            recv_c[:, d] = jnp.zeros(recv_c.shape[:1] + recv_c.shape[2:], BF)

    def pack(ref, phase):
        t_ref[...] = jnp.zeros_like(t_ref)
        for d, (dx, dy) in enumerate(DIRS):
            x = 1 if dx < 0 else bx
            r = 8 if dy < 0 else 8 + rows - S
            if dx and dy:
                t_ref[d, 0:S] = ref[x, r : r + S]
            elif dy:
                for i in range(bx):
                    t_ref[d, S * i : S * (i + 1)] = ref[i + 1, r : r + S]
            if dx and not dy:
                send_f[phase, d, 0:rows] = ref[x, 8 : 8 + rows].astype(BF)
            else:
                send_f[phase, d] = t_ref[d].astype(BF)

    def unpack(ref, phase):
        for d, (dx, dy) in enumerate(DIRS):
            x = 0 if dx < 0 else bx + 1
            r = 4 if dy < 0 else 8 + rows
            if dx and not dy:
                ref[x, 8 : 8 + rows] = recv_f[phase, d, 0:rows].astype(F32)
            elif dx:
                ref[x, r : r + S] = recv_f[phase, d, 0:16].astype(F32)[0:S]
            else:
                t_ref[d, 0:edge] = recv_f[phase, d, 0:edge].astype(F32)
                for i in range(bx):
                    ref[i + 1, r : r + S] = t_ref[d, S * i : S * (i + 1)]

    group_r = lax.broadcasted_iota(jnp.int32, (rows, flat), 0)
    group_c = lax.broadcasted_iota(jnp.int32, (rows, flat), 1)
    select = jnp.where(group_c // S == group_r, 1.0, 0.0).astype(BF)
    quarter = lax.broadcasted_iota(jnp.int32, (lanes, flat), 0) // width
    in_quarter = (lax.broadcasted_iota(jnp.int32, (lanes, flat), 1) % S == quarter).astype(F32).astype(BF)
    loads[0].wait()
    hl = flat // 2
    whole = x_ref[...].astype(F32).reshape(width * bx, flat)
    for k in range(2):
        v_ref[k] = whole[:, k * hl : (k + 1) * hl]
    for x in range(bx):
        one = jnp.concatenate([v_ref[k, pl.ds(x, width, stride=bx), :] for k in range(2)], axis=1).astype(BF)
        four = jnp.concatenate([one] * S, axis=0) * in_quarter
        f_ref[x + 1, 8 : 8 + rows] = dot(select, four, NT)

    pack(f_ref, 0)
    neighbours = sum(jnp.where(exists(d), 1, 0) for d in range(8))
    pl.semaphore_wait(barrier, neighbours)
    start_all(functools.partial(fine_copy, 0))

    def store_banded(ref, value):
        for k in range(9):
            ref[k // 3, :, (k % 3) * lanes : (k % 3 + 1) * lanes] = value[k]

    def permuted(ref):
        for k in range(S * S):
            parts = [perm_ref[pl.ds(S * k + z, width, stride=S * S * S), :] for z in range(S)]
            ref[k] = jnp.concatenate(parts, axis=0).astype(BF)

    loads[1].wait()
    store_banded(b1_ref, banded(wf_ref[...], 0, width))
    loads[2].wait()
    store_banded(b2_ref, banded(cw_ref[...], 0, width))
    store_banded(b3_ref, banded(cw_ref[...], 1, width))
    loads[3].wait()
    perm_ref[...] = dwo_ref[...].astype(F32)
    permuted(dw_ref)
    loads[4].wait()
    for k in range(perm_ref.shape[0] // cc):
        perm_ref[k * cc : (k + 1) * cc] = upo_ref[:, k * cc : (k + 1) * cc].astype(F32).T
    permuted(up_ref)

    def closing(ref, b_ref):
        zero = jnp.zeros((S, lanes), F32)
        for x in range(1, bx + 1):
            ref[x, 8 - S : 8] = zero
            ref[x, 8 + rows : 8 + rows + S] = zero
        for x in (0, bx + 1):
            a_ref[x] = jnp.zeros(a_ref.shape[1:], BF)
        spread(ref, a_ref, rows, lanes, 1, bx + 1)
        return fine(a_ref, b_ref, bx, rows).reshape(bx, rows, 2 * lanes)

    def beside(phase, b_ref):
        zero = jnp.zeros((S, lanes), F32)
        for x, dx in ((0, -1), (bx - 1, 1)):
            for k, dy in ((8 - S, -1), (8 + rows, 1)):
                h_ref[k : k + S] = recv_f[phase, DIRS.index((dx, dy)), 0:16].astype(F32)[0:S]
            h_ref[8 : 8 + rows] = recv_f[phase, DIRS.index((dx, 0)), 0:rows].astype(F32)
            acc_ref[x] += dot(jnp.concatenate(windows(h_ref, rows), axis=1), b_ref[1 + dx], NT)
        for r, dy in ((0, -1), (rows - S, 1)):
            h_ref[8 - S : 8] = zero
            h_ref[8 : 8 + edge] = recv_f[phase, DIRS.index((0, dy)), 0:edge].astype(F32)
            h_ref[8 + edge : 8 + edge + S] = zero
            b = jnp.concatenate([b_ref[k, :, (1 + dy) * lanes : (2 + dy) * lanes] for k in range(3)], axis=1)
            part = dot(jnp.concatenate(windows(h_ref, edge), axis=1), b, NT)
            for x in range(bx):
                acc_ref[x, r : r + S] += part[S * x : S * (x + 1)]

    recv_wait(fine_arrival(0))
    unpack(f_ref, 0)
    spread(f_ref, a_ref, rows, lanes, 0, bx + 2)
    skip = joined_z(fine(a_ref, b1_ref, bx, rows), lanes, width)
    skip = jnp.maximum(skip, 0.0).astype(BF).astype(F32)
    s_ref[1 : bx + 1, 8 : 8 + rows] = skip.reshape(bx, rows, lanes)
    pack(s_ref, 1)
    start_all(functools.partial(fine_copy, 1))

    pieces = []
    for ox in range(S):
        for half in range(2):
            group = []
            for a in range(ca):
                for b in range(cb):
                    r = 8 + b * S * S + half * 2 * S
                    group.append(s_ref[1 + S * a + ox, r : r + 2 * S])
            pieces.append(jnp.concatenate(group, axis=0).astype(BF))
    lhs = jnp.concatenate(pieces, axis=1)
    down = []
    for parity in range(2):
        down.append(
            jnp.concatenate([dw_ref[S * ox + 2 * half + parity] for ox in range(S) for half in range(2)], axis=0)
        )
    both = [dot(lhs, w).reshape(ca * cb, 2 * S, cc) for w in down]
    t_down = both[0][:, 0:S] + both[1][:, S : 2 * S]
    for a in range(ca):
        for b in range(cb):
            d_ref[a, S * b : S * (b + 1)] = t_down[a * cb + b]
    send_c[0] = d_ref[...].reshape(ca * crow, cc).astype(BF)
    start_all(functools.partial(coarse_copy, 0))

    acc_ref[...] = closing(s_ref, b2_ref)
    recv_wait(fine_arrival(1))
    beside(1, b2_ref)

    loads[5].wait()
    recv_wait(coarse_arrival(0))

    def place(phase):
        for d, (dx, dy) in enumerate(DIRS):
            c_ref[ca * (dx + 1) : ca * (dx + 2), 8 + crow * (dy + 1) : 8 + crow * (dy + 2)] = (
                recv_c[phase, d].astype(F32).reshape(ca, crow, cc)
            )
        c_ref[ca : 2 * ca, 8 + crow : 8 + 2 * crow] = send_c[phase].astype(F32).reshape(ca, crow, cc)

    place(0)
    for layer in range(layers):
        margin = layers - 1 - layer
        na, nb = ca + 2 * margin, cb + 2 * margin
        n = nb * S
        off = layer
        taps = []
        for da in range(3):
            for db in range(3):
                r = 8 + S * (off + db)
                taps.append(c_ref[off + da : off + da + na, r : r + n].astype(BF).reshape(na * n, cc))
        lhs = jnp.concatenate(taps, axis=1)
        terms = []
        for dz in range(3):
            rhs = jnp.concatenate([wc_ref[layer, 3 * t + dz] for t in range(9)], axis=1)
            terms.append(rhs)
        product = dot(lhs, jnp.concatenate(terms, axis=0), NT)
        zb = lax.broadcasted_iota(jnp.int32, (na * n, cc), 0) % S
        summed = (
            product[:, cc : 2 * cc]
            + jnp.where(zb != 0, pltpu.roll(product[:, :cc], 1, 0), 0.0)
            + jnp.where(zb != S - 1, pltpu.roll(product[:, 2 * cc :], na * n - 1, 0), 0.0)
        )
        summed = jnp.maximum(summed, 0.0).reshape(na, n, cc)
        ga = lax.broadcasted_iota(jnp.int32, (na, n, cc), 0) + ix * ca - margin
        gb = lax.broadcasted_iota(jnp.int32, (na, n, cc), 1) // S + iy * cb - margin
        keep = (ga >= 0) & (ga < nx * ca) & (gb >= 0) & (gb < ny * cb)
        summed = jnp.where(keep, summed, 0.0).astype(BF).astype(F32)
        c_ref[off + 1 : off + 1 + na, 8 + S * (off + 1) : 8 + S * (off + 1) + n] = summed
    cells = c_ref[ca : 2 * ca, 8 + crow : 8 + 2 * crow].reshape(ca * crow, cc).astype(BF)
    for ox in range(S):
        for oy in range(S):
            up = dot(cells, up_ref[S * ox + oy], NT).astype(BF).astype(F32)
            for a in range(ca):
                for b in range(cb):
                    y = S * b + oy
                    f_ref[S * a + ox + 1, 8 + S * y : 8 + S * (y + 1)] = up[a * crow + S * b : a * crow + S * (b + 1)]
    pack(f_ref, 2)
    start_all(functools.partial(fine_copy, 2))
    acc_ref[...] += closing(f_ref, b3_ref)
    recv_wait(fine_arrival(2))
    beside(2, b3_ref)

    total = joined_z(acc_ref[...].reshape(bx * rows, 2 * lanes), lanes, width).astype(BF)
    for x in range(bx):
        one = dot(total[x * rows : (x + 1) * rows], select, TN)
        picked = jnp.where(in_quarter > 0, one, 0.0)
        res = picked[0:width]
        for z in range(1, S):
            res = res + picked[z * width : (z + 1) * width]
        for k in range(2):
            o_ref[k, pl.ds(x, width, stride=bx), :] = res[:, k * hl : (k + 1) * hl]
    out_ref[...] = jnp.concatenate([o_ref[0], o_ref[1]], axis=1).astype(BF).reshape(width, bx, flat)

    for phase in range(3):
        sent_all(functools.partial(fine_copy, phase))
    sent_all(functools.partial(coarse_copy, 0))


def local(volume, w_first, down_weight, w_coarse, w_up, closing_weight):
    width, bx, flat = volume.shape
    by = flat // NZ
    lanes = S * width
    rows = by * (NZ // S)
    ca, crow = bx // S, by // S * S
    layers, _, cc, _ = w_coarse.shape
    slot = max(rows, S * bx)
    vmem = pl.BlockSpec(memory_space=pltpu.VMEM)
    return pl.pallas_call(
        functools.partial(kernel, ("sx", "sy")),
        out_shape=jax.ShapeDtypeStruct((width, bx, flat), BF),
        in_specs=[pl.BlockSpec(memory_space=pltpu.HBM)] * 6,
        out_specs=vmem,
        scratch_shapes=[
            pltpu.VMEM(volume.shape, BF),
            pltpu.VMEM(w_first.shape, BF),
            pltpu.VMEM(down_weight.shape, BF),
            pltpu.VMEM(w_coarse.shape, BF),
            pltpu.VMEM(w_up.shape, BF),
            pltpu.VMEM(closing_weight.shape, BF),
            pltpu.VMEM((2, width * bx, flat // 2), F32),
            pltpu.VMEM(down_weight.shape, F32),
            pltpu.VMEM((S * S, lanes, cc), BF),
            pltpu.VMEM((S * S, lanes, cc), BF),
            pltpu.VMEM((bx + 2, rows + 16, lanes), F32),
            pltpu.VMEM((bx + 2, rows + 16, lanes), F32),
            pltpu.VMEM((bx + 2, rows, 3 * lanes), BF),
            pltpu.VMEM((3, 2 * lanes, 3 * lanes), BF),
            pltpu.VMEM((3, 2 * lanes, 3 * lanes), BF),
            pltpu.VMEM((3, 2 * lanes, 3 * lanes), BF),
            pltpu.VMEM((bx, rows, 2 * lanes), F32),
            pltpu.VMEM((8, slot, lanes), F32),
            pltpu.VMEM((slot + 16, lanes), F32),
            pltpu.VMEM((3 * ca, 3 * crow + 16, cc), F32),
            pltpu.VMEM((ca, crow, cc), F32),
            pltpu.VMEM((2, width * bx, flat // 2), F32),
            pltpu.VMEM((3, 8, slot, lanes), BF),
            pltpu.VMEM((3, 8, slot, lanes), BF),
            pltpu.VMEM((1, ca * crow, cc), BF),
            pltpu.VMEM((1, 8, ca * crow, cc), BF),
            pltpu.SemaphoreType.DMA((6,)),
            pltpu.SemaphoreType.DMA((3, 8)),
            pltpu.SemaphoreType.DMA((3, 8)),
            pltpu.SemaphoreType.DMA((1, 8)),
            pltpu.SemaphoreType.DMA((1, 8)),
        ],
        compiler_params=pltpu.CompilerParams(
            collective_id=0, has_side_effects=True, vmem_limit_bytes=62 * 1024 * 1024
        ),
    )(volume, w_first, down_weight, w_coarse, w_up, closing_weight)


def solution(mesh):
    return jax.shard_map(
        local,
        mesh=mesh,
        in_specs=(P(None, "sx", "sy"), P(), P(), P(), P(), P()),
        out_specs=P(None, "sx", "sy"),
        check_vma=False,
    )
```

```python
import functools

import jax
import jax.numpy as jnp
from jax import lax
from jax.experimental import pallas as pl
from jax.experimental.pallas import tpu as pltpu
from jax.sharding import PartitionSpec as P

NZ = 16
S = 4
F32 = jnp.float32
BF = jnp.bfloat16
DIRS = [(dx, dy) for dx in (-1, 0, 1) for dy in (-1, 0, 1) if (dx, dy) != (0, 0)]
OPP = [DIRS.index((-dx, -dy)) for dx, dy in DIRS]
NT = (((1,), (1,)), ((), ()))
TN = (((0,), (0,)), ((), ()))


def dot(a, b, dims=(((1,), (0,)), ((), ()))):
    return lax.dot_general(a, b, dims, preferred_element_type=F32)


def banded(w, part, width):
    taps, out, inner = w.shape
    lanes = S * width
    shape = (inner, 2 * S * lanes)
    channel = lax.broadcasted_iota(jnp.int32, shape, 0)
    column = lax.broadcasted_iota(jnp.int32, shape, 1)
    block = column // lanes
    zi = column % lanes // width
    zo = jnp.where(block < S, block, jnp.where(block == S, S, jnp.where(block == 2 * S - 1, -1, 99)))
    same = channel == column % width + part * width
    w4 = w.reshape(taps // 3, 3, out, inner)
    total = None
    for tz in range(3):
        pick = jnp.where(same & (zi - zo + 1 == tz), 1.0, 0.0).astype(BF)
        term = dot(w4[:, tz].reshape(-1, inner), pick)
        total = term if total is None else total + term
    total = total.astype(BF).reshape(taps // 3, out, 2 * S * lanes)
    rows = [total[:, :, z * lanes : (z + 1) * lanes] for z in range(2 * S)]
    return jnp.concatenate(rows, axis=1)


def windows(v_ref, rows, *lead):
    return [v_ref[(*lead, slice(4 + S * k, 4 + S * k + rows))].astype(BF) for k in range(3)]


def spread(f_ref, a_ref, rows, lanes, lo, hi):
    def step(x, carry):
        for k, v in enumerate(windows(f_ref, rows, x)):
            a_ref[x, :, k * lanes : (k + 1) * lanes] = v
        return carry

    lax.fori_loop(lo, hi, step, 0)


def fine(a_ref, b_ref, bx, rows):
    a = jnp.concatenate([a_ref[k : k + bx].reshape(bx * rows, a_ref.shape[2]) for k in range(3)], axis=1)
    b = jnp.concatenate([b_ref[k] for k in range(3)], axis=1)
    return dot(a, b, NT)


def joined_z(total, lanes, width):
    n = total.shape[0]
    own, other = total[:, :lanes], total[:, lanes:]
    zb = lax.broadcasted_iota(jnp.int32, (n, lanes), 0) % S
    lane = lax.broadcasted_iota(jnp.int32, (n, lanes), 1)
    down = pltpu.roll(other, 1, 0)
    up = pltpu.roll(other, n - 1, 0)
    first = (lane < width) & (zb != 0)
    last = (lane >= lanes - width) & (zb != S - 1)
    return own + jnp.where(first, down, jnp.where(last, up, 0.0))


def kernel(
    axes, x_hbm, wf_hbm, dw_hbm, wc_hbm, up_hbm, cw_hbm, out_ref,
    x_ref, wf_ref, dwo_ref, wc_ref, upo_ref, cw_ref,
    v_ref, perm_ref, dw_ref, up_ref, f_ref, s_ref, a_ref, b1_ref, b2_ref, b3_ref, acc_ref, t_ref, h_ref,
    c_ref, d_ref, send_f, recv_f, send_c, recv_c, wsem, ssem_f, rsem_f, ssem_c, rsem_c,
):
    ax, ay = axes
    nx, ny = lax.axis_size(ax), lax.axis_size(ay)
    ix, iy = lax.axis_index(ax), lax.axis_index(ay)
    width, bx, flat = x_ref.shape
    by = flat // NZ
    lanes = S * width
    rows = by * (NZ // S)
    ca, cb = bx // S, by // S
    cc = wc_ref.shape[2]
    layers = wc_ref.shape[0]
    crow = cb * S
    edge = bx * S

    pairs = [(x_hbm, x_ref), (wf_hbm, wf_ref), (cw_hbm, cw_ref), (dw_hbm, dwo_ref), (up_hbm, upo_ref), (wc_hbm, wc_ref)]
    loads = [pltpu.make_async_copy(src, dst, wsem.at[k]) for k, (src, dst) in enumerate(pairs)]
    for load in loads:
        load.start()

    def exists(d):
        dx, dy = DIRS[d]
        ok = ix >= 0
        if dx:
            ok = ok & (ix + dx >= 0) & (ix + dx < nx)
        if dy:
            ok = ok & (iy + dy >= 0) & (iy + dy < ny)
        return ok

    def target(d):
        dx, dy = DIRS[d]
        return (ix + dx, iy + dy)

    barrier = pltpu.get_barrier_semaphore()
    for d in range(8):
        @pl.when(exists(d))
        def _(d=d):
            pl.semaphore_signal(barrier, inc=1, device_id=target(d), device_id_type=pl.DeviceIdType.MESH)

    def fine_copy(phase, d):
        count = 16 if DIRS[d][0] and DIRS[d][1] else (rows if DIRS[d][0] else edge)
        return pltpu.make_async_remote_copy(
            src_ref=send_f.at[phase, d, pl.ds(0, count)],
            dst_ref=recv_f.at[phase, OPP[d], pl.ds(0, count)],
            send_sem=ssem_f.at[phase, d],
            recv_sem=rsem_f.at[phase, OPP[d]],
            device_id=target(d),
            device_id_type=pl.DeviceIdType.MESH,
        )

    def coarse_copy(phase, d):
        return pltpu.make_async_remote_copy(
            src_ref=send_c.at[phase],
            dst_ref=recv_c.at[phase, OPP[d]],
            send_sem=ssem_c.at[phase, d],
            recv_sem=rsem_c.at[phase, OPP[d]],
            device_id=target(d),
            device_id_type=pl.DeviceIdType.MESH,
        )

    def each(make, act):
        for d in range(8):
            @pl.when(exists(d))
            def _(d=d):
                act(make(d), d)

    def start_all(make):
        each(make, lambda c, d: c.start())

    def sent_all(make):
        each(make, lambda c, d: c.wait_send())

    def recv_wait(copy_of):
        for d in range(8):
            @pl.when(exists(d))
            def _(d=d):
                copy_of(d).wait_recv()

    def fine_arrival(phase):
        def make(d):
            count = 16 if DIRS[d][0] and DIRS[d][1] else (rows if DIRS[d][0] else edge)
            return pltpu.make_async_remote_copy(
                src_ref=send_f.at[phase, d, pl.ds(0, count)],
                dst_ref=recv_f.at[phase, d, pl.ds(0, count)],
                send_sem=ssem_f.at[phase, d],
                recv_sem=rsem_f.at[phase, d],
                device_id=target(d),
                device_id_type=pl.DeviceIdType.MESH,
            )
        return make

    def coarse_arrival(phase):
        def make(d):
            return pltpu.make_async_remote_copy(
                src_ref=send_c.at[phase],
                dst_ref=recv_c.at[phase, d],
                send_sem=ssem_c.at[phase, d],
                recv_sem=rsem_c.at[phase, d],
                device_id=target(d),
                device_id_type=pl.DeviceIdType.MESH,
            )
        return make

    for d in range(8):
        @pl.when(jnp.logical_not(exists(d)))
        def _(d=d):
            recv_f[:, d] = jnp.zeros(recv_f.shape[:1] + recv_f.shape[2:], BF)
            recv_c[:, d] = jnp.zeros(recv_c.shape[:1] + recv_c.shape[2:], BF)

    def pack(ref, phase):
        t_ref[...] = jnp.zeros_like(t_ref)
        for d, (dx, dy) in enumerate(DIRS):
            x = 1 if dx < 0 else bx
            r = 8 if dy < 0 else 8 + rows - S
            if dx and dy:
                t_ref[d, 0:S] = ref[x, r : r + S]
            elif dy:
                for i in range(bx):
                    t_ref[d, S * i : S * (i + 1)] = ref[i + 1, r : r + S]
            if dx and not dy:
                send_f[phase, d, 0:rows] = ref[x, 8 : 8 + rows].astype(BF)
            else:
                send_f[phase, d] = t_ref[d].astype(BF)

    def unpack(ref, phase):
        for d, (dx, dy) in enumerate(DIRS):
            x = 0 if dx < 0 else bx + 1
            r = 4 if dy < 0 else 8 + rows
            if dx and not dy:
                ref[x, 8 : 8 + rows] = recv_f[phase, d, 0:rows].astype(F32)
            elif dx:
                ref[x, r : r + S] = recv_f[phase, d, 0:16].astype(F32)[0:S]
            else:
                t_ref[d, 0:edge] = recv_f[phase, d, 0:edge].astype(F32)
                for i in range(bx):
                    ref[i + 1, r : r + S] = t_ref[d, S * i : S * (i + 1)]

    group_r = lax.broadcasted_iota(jnp.int32, (rows, flat), 0)
    group_c = lax.broadcasted_iota(jnp.int32, (rows, flat), 1)
    select = jnp.where(group_c // S == group_r, 1.0, 0.0).astype(BF)
    quarter = lax.broadcasted_iota(jnp.int32, (lanes, flat), 0) // width
    in_quarter = (lax.broadcasted_iota(jnp.int32, (lanes, flat), 1) % S == quarter).astype(F32).astype(BF)
    loads[0].wait()
    hl = flat // 2
    whole = x_ref[...].astype(F32).reshape(width * bx, flat)
    for k in range(2):
        v_ref[k] = whole[:, k * hl : (k + 1) * hl]
    for x in range(bx):
        one = jnp.concatenate([v_ref[k, pl.ds(x, width, stride=bx), :] for k in range(2)], axis=1).astype(BF)
        four = jnp.concatenate([one] * S, axis=0) * in_quarter
        f_ref[x + 1, 8 : 8 + rows] = dot(select, four, NT)

    pack(f_ref, 0)
    neighbours = sum(jnp.where(exists(d), 1, 0) for d in range(8))
    pl.semaphore_wait(barrier, neighbours)
    start_all(functools.partial(fine_copy, 0))

    def store_banded(ref, value):
        for k in range(9):
            ref[k // 3, :, (k % 3) * lanes : (k % 3 + 1) * lanes] = value[k]

    def permuted(ref):
        for k in range(S * S):
            parts = [perm_ref[pl.ds(S * k + z, width, stride=S * S * S), :] for z in range(S)]
            ref[k] = jnp.concatenate(parts, axis=0).astype(BF)

    loads[1].wait()
    store_banded(b1_ref, banded(wf_ref[...], 0, width))
    loads[2].wait()
    store_banded(b2_ref, banded(cw_ref[...], 0, width))
    store_banded(b3_ref, banded(cw_ref[...], 1, width))
    loads[3].wait()
    perm_ref[...] = dwo_ref[...].astype(F32)
    permuted(dw_ref)
    loads[4].wait()
    for k in range(perm_ref.shape[0] // cc):
        perm_ref[k * cc : (k + 1) * cc] = upo_ref[:, k * cc : (k + 1) * cc].astype(F32).T
    permuted(up_ref)

    def closing(ref, b_ref):
        zero = jnp.zeros((S, lanes), F32)
        for x in range(1, bx + 1):
            ref[x, 8 - S : 8] = zero
            ref[x, 8 + rows : 8 + rows + S] = zero
        for x in (0, bx + 1):
            a_ref[x] = jnp.zeros(a_ref.shape[1:], BF)
        spread(ref, a_ref, rows, lanes, 1, bx + 1)
        return fine(a_ref, b_ref, bx, rows).reshape(bx, rows, 2 * lanes)

    def beside(phase, b_ref):
        zero = jnp.zeros((S, lanes), F32)
        for x, dx in ((0, -1), (bx - 1, 1)):
            for k, dy in ((8 - S, -1), (8 + rows, 1)):
                h_ref[k : k + S] = recv_f[phase, DIRS.index((dx, dy)), 0:16].astype(F32)[0:S]
            h_ref[8 : 8 + rows] = recv_f[phase, DIRS.index((dx, 0)), 0:rows].astype(F32)
            acc_ref[x] += dot(jnp.concatenate(windows(h_ref, rows), axis=1), b_ref[1 + dx], NT)
        for r, dy in ((0, -1), (rows - S, 1)):
            h_ref[8 - S : 8] = zero
            h_ref[8 : 8 + edge] = recv_f[phase, DIRS.index((0, dy)), 0:edge].astype(F32)
            h_ref[8 + edge : 8 + edge + S] = zero
            b = jnp.concatenate([b_ref[k, :, (1 + dy) * lanes : (2 + dy) * lanes] for k in range(3)], axis=1)
            part = dot(jnp.concatenate(windows(h_ref, edge), axis=1), b, NT)
            for x in range(bx):
                acc_ref[x, r : r + S] += part[S * x : S * (x + 1)]

    recv_wait(fine_arrival(0))
    unpack(f_ref, 0)
    spread(f_ref, a_ref, rows, lanes, 0, bx + 2)
    skip = joined_z(fine(a_ref, b1_ref, bx, rows), lanes, width)
    skip = jnp.maximum(skip, 0.0).astype(BF).astype(F32)
    s_ref[1 : bx + 1, 8 : 8 + rows] = skip.reshape(bx, rows, lanes)
    pack(s_ref, 1)
    start_all(functools.partial(fine_copy, 1))

    pieces = []
    for ox in range(S):
        for half in range(2):
            group = []
            for a in range(ca):
                for b in range(cb):
                    r = 8 + b * S * S + half * 2 * S
                    group.append(s_ref[1 + S * a + ox, r : r + 2 * S])
            pieces.append(jnp.concatenate(group, axis=0).astype(BF))
    lhs = jnp.concatenate(pieces, axis=1)
    down = []
    for parity in range(2):
        down.append(
            jnp.concatenate([dw_ref[S * ox + 2 * half + parity] for ox in range(S) for half in range(2)], axis=0)
        )
    both = [dot(lhs, w).reshape(ca * cb, 2 * S, cc) for w in down]
    t_down = both[0][:, 0:S] + both[1][:, S : 2 * S]
    for a in range(ca):
        for b in range(cb):
            d_ref[a, S * b : S * (b + 1)] = t_down[a * cb + b]
    send_c[0] = d_ref[...].reshape(ca * crow, cc).astype(BF)
    start_all(functools.partial(coarse_copy, 0))

    acc_ref[...] = closing(s_ref, b2_ref)
    recv_wait(fine_arrival(1))
    beside(1, b2_ref)

    loads[5].wait()
    recv_wait(coarse_arrival(0))

    def place(phase):
        for d, (dx, dy) in enumerate(DIRS):
            c_ref[ca * (dx + 1) : ca * (dx + 2), 8 + crow * (dy + 1) : 8 + crow * (dy + 2)] = (
                recv_c[phase, d].astype(F32).reshape(ca, crow, cc)
            )
        c_ref[ca : 2 * ca, 8 + crow : 8 + 2 * crow] = send_c[phase].astype(F32).reshape(ca, crow, cc)

    place(0)
    for layer in range(layers):
        margin = layers - 1 - layer
        na, nb = ca + 2 * margin, cb + 2 * margin
        n = nb * S
        off = layer
        taps = []
        for da in range(3):
            for db in range(3):
                r = 8 + S * (off + db)
                taps.append(c_ref[off + da : off + da + na, r : r + n].astype(BF).reshape(na * n, cc))
        lhs = jnp.concatenate(taps, axis=1)
        terms = []
        for dz in range(3):
            rhs = jnp.concatenate([wc_ref[layer, 3 * t + dz] for t in range(9)], axis=1)
            terms.append(rhs)
        product = dot(lhs, jnp.concatenate(terms, axis=0), NT)
        zb = lax.broadcasted_iota(jnp.int32, (na * n, cc), 0) % S
        summed = (
            product[:, cc : 2 * cc]
            + jnp.where(zb != 0, pltpu.roll(product[:, :cc], 1, 0), 0.0)
            + jnp.where(zb != S - 1, pltpu.roll(product[:, 2 * cc :], na * n - 1, 0), 0.0)
        )
        summed = jnp.maximum(summed, 0.0).reshape(na, n, cc)
        ga = lax.broadcasted_iota(jnp.int32, (na, n, cc), 0) + ix * ca - margin
        gb = lax.broadcasted_iota(jnp.int32, (na, n, cc), 1) // S + iy * cb - margin
        keep = (ga >= 0) & (ga < nx * ca) & (gb >= 0) & (gb < ny * cb)
        summed = jnp.where(keep, summed, 0.0).astype(BF).astype(F32)
        c_ref[off + 1 : off + 1 + na, 8 + S * (off + 1) : 8 + S * (off + 1) + n] = summed
    cells = c_ref[ca : 2 * ca, 8 + crow : 8 + 2 * crow].reshape(ca * crow, cc).astype(BF)
    for ox in range(S):
        for oy in range(S):
            up = dot(cells, up_ref[S * ox + oy], NT).astype(BF).astype(F32)
            for a in range(ca):
                for b in range(cb):
                    y = S * b + oy
                    f_ref[S * a + ox + 1, 8 + S * y : 8 + S * (y + 1)] = up[a * crow + S * b : a * crow + S * (b + 1)]
    pack(f_ref, 2)
    start_all(functools.partial(fine_copy, 2))
    acc_ref[...] += closing(f_ref, b3_ref)
    recv_wait(fine_arrival(2))
    beside(2, b3_ref)

    total = joined_z(acc_ref[...].reshape(bx * rows, 2 * lanes), lanes, width).astype(BF)
    out_ref[...] = total

    for phase in range(3):
        sent_all(functools.partial(fine_copy, phase))
    sent_all(functools.partial(coarse_copy, 0))


def relayout(total_ref, out_ref, o_ref):
    width, bx, flat = out_ref.shape
    rows, lanes, hl = flat // S, S * width, flat // 2
    group_r = lax.broadcasted_iota(jnp.int32, (rows, flat), 0)
    group_c = lax.broadcasted_iota(jnp.int32, (rows, flat), 1)
    select = jnp.where(group_c // S == group_r, 1.0, 0.0).astype(BF)
    quarter = lax.broadcasted_iota(jnp.int32, (lanes, flat), 0) // width
    in_quarter = lax.broadcasted_iota(jnp.int32, (lanes, flat), 1) % S == quarter
    for x in range(bx):
        one = dot(total_ref[x * rows : (x + 1) * rows], select, TN)
        picked = jnp.where(in_quarter, one, 0.0)
        res = picked[0:width]
        for z in range(1, S):
            res = res + picked[z * width : (z + 1) * width]
        for k in range(2):
            o_ref[k, pl.ds(x, width, stride=bx), :] = res[:, k * hl : (k + 1) * hl]
    out_ref[...] = jnp.concatenate([o_ref[0], o_ref[1]], axis=1).astype(BF).reshape(width, bx, flat)


def local(volume, w_first, down_weight, w_coarse, w_up, closing_weight):
    width, bx, flat = volume.shape
    by = flat // NZ
    lanes = S * width
    rows = by * (NZ // S)
    ca, crow = bx // S, by // S * S
    layers, _, cc, _ = w_coarse.shape
    slot = max(rows, S * bx)
    vmem = pl.BlockSpec(memory_space=pltpu.VMEM)
    sums = pl.pallas_call(
        functools.partial(kernel, ("sx", "sy")),
        out_shape=jax.ShapeDtypeStruct((bx * rows, lanes), BF),
        in_specs=[pl.BlockSpec(memory_space=pltpu.HBM)] * 6,
        out_specs=vmem,
        scratch_shapes=[
            pltpu.VMEM(volume.shape, BF),
            pltpu.VMEM(w_first.shape, BF),
            pltpu.VMEM(down_weight.shape, BF),
            pltpu.VMEM(w_coarse.shape, BF),
            pltpu.VMEM(w_up.shape, BF),
            pltpu.VMEM(closing_weight.shape, BF),
            pltpu.VMEM((2, width * bx, flat // 2), F32),
            pltpu.VMEM(down_weight.shape, F32),
            pltpu.VMEM((S * S, lanes, cc), BF),
            pltpu.VMEM((S * S, lanes, cc), BF),
            pltpu.VMEM((bx + 2, rows + 16, lanes), F32),
            pltpu.VMEM((bx + 2, rows + 16, lanes), F32),
            pltpu.VMEM((bx + 2, rows, 3 * lanes), BF),
            pltpu.VMEM((3, 2 * lanes, 3 * lanes), BF),
            pltpu.VMEM((3, 2 * lanes, 3 * lanes), BF),
            pltpu.VMEM((3, 2 * lanes, 3 * lanes), BF),
            pltpu.VMEM((bx, rows, 2 * lanes), F32),
            pltpu.VMEM((8, slot, lanes), F32),
            pltpu.VMEM((slot + 16, lanes), F32),
            pltpu.VMEM((3 * ca, 3 * crow + 16, cc), F32),
            pltpu.VMEM((ca, crow, cc), F32),
            pltpu.VMEM((3, 8, slot, lanes), BF),
            pltpu.VMEM((3, 8, slot, lanes), BF),
            pltpu.VMEM((1, ca * crow, cc), BF),
            pltpu.VMEM((1, 8, ca * crow, cc), BF),
            pltpu.SemaphoreType.DMA((6,)),
            pltpu.SemaphoreType.DMA((3, 8)),
            pltpu.SemaphoreType.DMA((3, 8)),
            pltpu.SemaphoreType.DMA((1, 8)),
            pltpu.SemaphoreType.DMA((1, 8)),
        ],
        compiler_params=pltpu.CompilerParams(
            collective_id=0, has_side_effects=True, vmem_limit_bytes=62 * 1024 * 1024
        ),
    )(volume, w_first, down_weight, w_coarse, w_up, closing_weight)
    return pl.pallas_call(
        relayout,
        out_shape=jax.ShapeDtypeStruct((width, bx, flat), BF),
        in_specs=[vmem],
        out_specs=vmem,
        scratch_shapes=[pltpu.VMEM((2, width * bx, flat // 2), F32)],
        compiler_params=pltpu.CompilerParams(vmem_limit_bytes=16 * 1024 * 1024),
    )(sums)


def solution(mesh):
    return jax.shard_map(
        local,
        mesh=mesh,
        in_specs=(P(None, "sx", "sy"), P(), P(), P(), P(), P()),
        out_specs=P(None, "sx", "sy"),
        check_vma=False,
    )
```
